512 devices in a mesh: layer: 2 (over core), row: 64 (over z, y), rep: 4 (over x).
Axes of the slice: x: 4, y: 4, z: 16, core: 2. Of those that a mesh axis runs over, the one named last changes fastest.
Arguments:
- features: bfloat16 [32768, 256], P(('row', 'rep')), may hold values from -6 to 6
- class_ids: int32 [32768], P(('row', 'rep')), may hold values from 0 to 256
- label_table: bfloat16 [256, 256], replicated, may hold values from -3 to 3
- self_weight: bfloat16 [2, 256, 256], P('layer'), may hold values from -0.375 to 0.375
- neighbor_weight: bfloat16 [2, 256, 256], P('layer'), may hold values from -0.375 to 0.375
- norm_scale: float32 [256], replicated, may hold values from 0.1 to 1.9
- tile_values: bfloat16 [64, 4, 32, 128, 128], P('row', 'rep')
- tile_block_row: int32 [64, 4, 32], P('row', 'rep'), may hold values from 0 to 3, as said below
- tile_section: int32 [64, 4, 32], P('row', 'rep'), may hold values from 0 to 63
- tile_count: int32 [64, 4], P('row', 'rep'), may hold values from 4 to 32, as said below
Outputs:
- hidden_states: bfloat16 [2, 32768, 256], P('layer', ('row', 'rep'))
The draws below stay inside these ranges and needn't reach their ends.
Inputs may be any that keep to these rules, and one draw needn't show every extreme that they name: `class_ids`: 256 marks a node without a label. `tile_block_row`: slots 0 to 3 of every device name block rows 0 to 3 in order. `tile_count`: at least 4; 32 on some device.
All inputs are finite; a program needn't handle non-finite values.
Results may differ from the reference program's by a relative error of at most 0.0052.
Values may be sent and summed in bfloat16 or wider, within the bound.
A program may use at most 64 MiB of HBM per device.

```python
import math
import jax
import jax.numpy as jnp
from jax import lax

F = 256
CLASSES = 256
BLOCK = 128
K_DEV = 32
GROUPS = 64
SPLITS = 4
NODES = 32768


def draw_tile_values(key, part):
    first_key, second_key = jax.random.split(key)
    shape = (GROUPS, SPLITS, K_DEV, BLOCK, BLOCK)
    row_scale = jnp.exp(jax.random.uniform(first_key, (GROUPS, SPLITS, K_DEV, BLOCK, 1), jnp.float32, math.log(0.1), 0.0))
    entries = jnp.exp(jax.random.uniform(second_key, shape, jnp.float32, math.log(0.05), 0.0))
    return (entries * row_scale).astype(jnp.bfloat16)


def draw_tile_block_row(key, part):
    drawn = jax.random.randint(key, (GROUPS, SPLITS, K_DEV), 0, SPLITS)
    slot_ids = jnp.arange(K_DEV, dtype=jnp.int32)
    return jnp.where(slot_ids[None, None, :] < SPLITS, slot_ids[None, None, :], drawn).astype(jnp.int32)


def draw_tile_count(key, part):
    first_key, second_key = jax.random.split(key)
    counts = jax.random.randint(first_key, (GROUPS * SPLITS,), SPLITS, K_DEV + 1)
    chosen = jax.random.randint(second_key, (), 0, GROUPS * SPLITS)
    flat = jnp.where(jnp.arange(GROUPS * SPLITS, dtype=jnp.int32) == chosen, K_DEV, counts)
    return flat.reshape(GROUPS, SPLITS).astype(jnp.int32)


def set_ends(values, key, low, largest):
    index_at = [jax.random.randint(jax.random.fold_in(key, axis), (), 0, length) for axis, length in enumerate(values.shape)]
    widest = values.shape.index(max(values.shape))
    neighbour = index_at[:widest] + [(index_at[widest] + 1) % values.shape[widest]] + index_at[widest + 1:]
    return values.at[tuple(index_at)].set(low).at[tuple(neighbour)].set(largest)


def levels(rng, dims, shards, smallest, largest):
    def one(axis_at, shards_of):
        steps = jax.random.uniform(jax.random.fold_in(jax.random.fold_in(rng, 6), axis_at), (shards_of,), jnp.float32, smallest / len(shards), largest / len(shards))
        return jnp.repeat(jnp.exp(steps), dims[axis_at] // shards_of).reshape((-1,) + (1,) * (len(dims) - axis_at - 1))

    level = one(*shards[0])
    for cut in shards[1:]:
        level = level * one(*cut)
    return level


def normal_values(stream_key, dims, width, most, cuts=(), kind=jnp.bfloat16):
    values = width * jax.random.normal(stream_key, dims, jnp.float32)
    if cuts:
        values = values * levels(stream_key, dims, cuts, -0.22, 0.18)
    return jnp.clip(values, -most, most).astype(kind)


def setup_inputs(seed: int = 0) -> dict:
    arg_keys = jax.random.split(jax.random.key(seed), 11)
    features = normal_values(arg_keys[0], (NODES, F), 1.0, 6.0, ((0, 256),))
    class_ids = set_ends(jax.random.randint(arg_keys[1], (NODES,), 0, CLASSES + 1), jax.random.fold_in(arg_keys[1], 1), 0, CLASSES).astype(jnp.int32)
    label_table = normal_values(arg_keys[2], (CLASSES, F), 0.5, 3.0)
    self_weight = normal_values(arg_keys[3], (2, F, F), F ** -0.5, 0.375, ((0, 2),))
    neighbor_weight = normal_values(arg_keys[4], (2, F, F), F ** -0.5, 0.375, ((0, 2),))
    norm_scale = jnp.clip(1.0 + 0.18 * jax.random.normal(arg_keys[5], (F,), jnp.float32), 0.1, 1.9)
    tile_values = draw_tile_values(jax.random.fold_in(arg_keys[10], 71), 0)
    tile_block_row = draw_tile_block_row(jax.random.fold_in(arg_keys[10], 71), 0)
    tile_section = set_ends(jax.random.randint(arg_keys[8], (GROUPS, SPLITS, K_DEV), 0, GROUPS), jax.random.fold_in(arg_keys[8], 1), 0, GROUPS - 1).astype(jnp.int32)
    tile_count = draw_tile_count(jax.random.fold_in(arg_keys[10], 71), 0)
    return {"features": features, "class_ids": class_ids, "label_table": label_table, "self_weight": self_weight, "neighbor_weight": neighbor_weight, "norm_scale": norm_scale, "tile_values": tile_values, "tile_block_row": tile_block_row, "tile_section": tile_section, "tile_count": tile_count}


def aggregate(current, tile_values, tile_block_row, tile_section, tile_count):
    groups, splits, slot_total = tile_section.shape
    tile_edge = tile_values.shape[-1]
    hidden_dim = current.shape[1]
    blocked = current.astype(jnp.float32).reshape(groups, splits, tile_edge, hidden_dim)
    slot_ids = jnp.arange(slot_total, dtype=jnp.int32)
    targets = jnp.arange(splits, dtype=jnp.int32)

    def one_group(pieces):
        tile_data, tile_rows, tile_cols, filled = pieces
        running = jnp.zeros((splits, tile_edge, hidden_dim), jnp.float32)
        degree = jnp.zeros((splits, tile_edge), jnp.float32)
        for split_no in range(splits):
            live = (slot_ids < filled[split_no]).astype(jnp.float32)
            sources = blocked[tile_cols[split_no], split_no]
            entries = tile_data[split_no].astype(jnp.float32)
            products = jnp.einsum('kab,kbf->kaf', entries, sources, precision=lax.Precision.HIGHEST)
            onto_rows = (tile_rows[split_no][None, :] == targets[:, None]).astype(jnp.float32) * live[None, :]
            running = running + jnp.einsum('sk,kaf->saf', onto_rows, products, precision=lax.Precision.HIGHEST)
            degree = degree + jnp.einsum('sk,ka->sa', onto_rows, lax.optimization_barrier(jnp.sum(entries, axis=-1)), precision=lax.Precision.HIGHEST)
        return (running.reshape(splits * tile_edge, hidden_dim), degree.reshape(splits * tile_edge))
    totals, degrees = lax.map(one_group, (tile_values, tile_block_row, tile_section, tile_count))
    return (totals.reshape(-1, hidden_dim), degrees.reshape(-1))

def settle_norm(mixture, norm_scale):
    active = jnp.maximum(mixture, 0.0)
    center = active - lax.optimization_barrier(jnp.mean(active, axis=-1, keepdims=True))
    spread = lax.optimization_barrier(jnp.mean(center * center, axis=-1, keepdims=True))
    return (center * lax.rsqrt(spread + 1e-05) * norm_scale).astype(jnp.bfloat16)

def reference(features, class_ids, label_table, self_weight, neighbor_weight, norm_scale, tile_values, tile_block_row, tile_section, tile_count):
    classes = label_table.shape[0]
    one_hot = (class_ids[:, None] == jnp.arange(classes, dtype=jnp.int32)[None, :]).astype(jnp.bfloat16)
    inputs = (features.astype(jnp.float32) + jnp.dot(one_hot, label_table, preferred_element_type=jnp.float32)).astype(jnp.bfloat16)
    summed, degree = aggregate(inputs, tile_values, tile_block_row, tile_section, tile_count)
    neighbor = (summed * lax.rsqrt(degree)[:, None]).astype(jnp.bfloat16)
    mixture = jnp.dot(inputs, self_weight[0], preferred_element_type=jnp.float32) + jnp.dot(neighbor, neighbor_weight[0], preferred_element_type=jnp.float32)
    first = settle_norm(mixture, norm_scale)
    summed_two, degree_two = aggregate(first, tile_values, tile_block_row, tile_section, tile_count)
    neighbor_two = (summed_two * lax.rsqrt(degree)[:, None]).astype(jnp.bfloat16)
    mixture_two = jnp.dot(first, self_weight[1], preferred_element_type=jnp.float32) + jnp.dot(neighbor_two, neighbor_weight[1], preferred_element_type=jnp.float32)
    logits = mixture_two.astype(jnp.bfloat16)
    return jnp.stack([first, logits])
```

```python
import functools

import jax
import jax.numpy as jnp
from jax import lax
from jax.experimental import pallas as pl
from jax.experimental.pallas import tpu as pltpu
from jax.sharding import PartitionSpec as P

MESH = pl.DeviceIdType.MESH
RING_Y = 4
ROWS_A = 48
F32 = jnp.float32
BF16 = jnp.bfloat16


def kernel(
    ring_z,
    reps,
    features,
    class_ids,
    label_table,
    self_weight,
    neighbor_weight,
    norm_scale,
    tile_values,
    block_row,
    section,
    count,
    out,
    tiles,
    placed,
    panels,
    first_a,
    first_b,
    second_a,
    second_b,
    weights,
    nodes,
    own_product,
    to_send,
    arrived,
    degree,
    degree_arrived,
    send_sem,
    recv_sem,
    tile_sem,
):
    slots = tiles.shape[0]
    edge = tiles.shape[1]
    parts_a, parts_b = (first_a, second_a), (first_b, second_b)
    rows_a, half_f = first_a.shape[1:]
    rows_b = first_b.shape[2]
    half_z = ring_z // 2
    core = lax.axis_index("layer")
    row = lax.axis_index("row")
    rep = lax.axis_index("rep")
    z, y = row // RING_Y, row % RING_Y

    def device(dz=0, dy=0, dr=0, dc=0):
        to_row = ((z + dz + ring_z) % ring_z) * RING_Y + (y + dy + RING_Y) % RING_Y
        return ((core + dc) % 2, to_row, (rep + dr) % reps)

    def z_slot(d):
        d = d % ring_z
        if d < half_z:
            return 2 * d
        return ring_z - 1 if d == half_z else 2 * (ring_z - d) - 1

    started = []

    def send(src, dst, device_id):
        at = len(started)
        copy = pltpu.make_async_remote_copy(
            src_ref=src,
            dst_ref=dst,
            send_sem=send_sem.at[at],
            recv_sem=recv_sem.at[at],
            device_id=device_id,
            device_id_type=MESH,
        )
        copy.start()
        started.append(copy)
        return copy

    tile_copy = pltpu.make_async_copy(tile_values.at[0, 0], tiles, tile_sem)
    tile_copy.start()

    barrier = pltpu.get_barrier_semaphore()
    friends = [device(dz=1), device(dz=-1), device(dy=1), device(dy=-1), device(dy=2), device(dc=1)]
    for j in range(1, reps):
        friends += [device(dr=j), device(dr=j, dc=1)]
    for friend in friends:
        pl.semaphore_signal(barrier, inc=1, device_id=friend, device_id_type=MESH)

    classes = label_table.shape[0]
    one_hot = (
        lax.broadcasted_iota(jnp.int32, (classes, edge), 0) == class_ids[...]
    ).astype(F32).astype(BF16)
    labels = lax.dot_general(
        one_hot, label_table[...], (((0,), (0,)), ((), ())), preferred_element_type=F32
    )
    inputs = (features[...].astype(F32) + labels).astype(BF16)
    nodes[0] = inputs

    def own_half(whole):
        return jnp.where(core == 0, whole[:, :half_f].astype(F32), whole[:, half_f:].astype(F32)).astype(BF16)

    def gather(layer, whole, work):
        a, b = parts_a[layer], parts_b[layer]
        mine = own_half(whole)
        a[0] = mine[:rows_a]
        b[0, 0] = mine[rows_a:]
        if layer == 0:
            pl.semaphore_wait(barrier, len(friends))

        def b_ring(s):
            cut = 48 if rows_b >= 64 else rows_b // 2
            if s < half_z:
                up, down = slice(None), slice(None)
            else:
                up, down = slice(0, cut), slice(cut, rows_b)
            return (
                send(b.at[0, z_slot(1 - s), up], b.at[0, z_slot(-s), up], device(dz=1)),
                send(b.at[0, z_slot(s - 1), down], b.at[0, z_slot(s), down], device(dz=-1)),
            )

        def a_ring(s):
            def block(d, part):
                at = z_slot(d) * RING_Y
                if s < half_z:
                    return a.at[pl.ds(at, RING_Y)]
                return a.at[pl.ds(at + part * (RING_Y // 2), RING_Y // 2)]

            return (
                send(block(1 - s, 0), block(-s, 0), device(dz=1)),
                send(block(s - 1, 1), block(s, 1), device(dz=-1)),
            )

        def b_side(s):
            if s == 0:
                at = pl.ds(0, 1)
            elif s < half_z:
                at = pl.ds(2 * s - 1, 2)
            else:
                at = pl.ds(ring_z - 1, 1)
            copies = [
                send(b.at[0, at], b.at[RING_Y - 1, at], device(dy=1)),
                send(b.at[0, at], b.at[1, at], device(dy=-1)),
            ]
            if s == half_z:
                copies.append(send(b.at[0, at], b.at[2, at], device(dy=2)))
            return copies

        def b_far(s):
            copies = [send(b.at[RING_Y - 1, max(2 * s - 1, 0)], b.at[2, max(2 * s - 1, 0)], device(dy=1))]
            if s > 0:
                copies.append(send(b.at[1, 2 * s], b.at[2, 2 * s], device(dy=-1)))
            return copies

        a_side = [
            send(a.at[0], a.at[(RING_Y - dy) % RING_Y], device(dy=dy)) for dy in (1, -1, 2)
        ]
        b_now = b_ring(1)
        side = b_side(0)
        last = []
        for copy in a_side:
            copy.wait_recv()
        a_now = a_ring(1)
        work(0)
        for s in range(1, half_z + 1):
            for copy in b_now:
                copy.wait_recv()
            if s < half_z:
                b_now = b_ring(s + 1)
            side_next = b_side(s)
            for copy in a_now:
                copy.wait_recv()
            if s < half_z:
                a_now = a_ring(s + 1)
            for copy in side:
                copy.wait_recv()
            last += b_far(s - 1)
            side = side_next
            work(s)
        for copy in side + last:
            copy.wait_recv()

    filled = count[0, 0]
    targets = [(block_row[0, 0, k] - rep + reps) % reps for k in range(slots)]
    per_step = max(slots // 4, 1)
    ones = jnp.ones((per_step * edge, half_f), BF16)
    hidden = []

    def place(step):
        for k in range(step * per_step, (step + 1) * per_step):
            tile = tiles[k]
            for j in range(reps):
                keep = jnp.logical_and(targets[k] == j, k < filled)
                placed[pl.ds(j * edge, edge), pl.ds(k * edge, edge)] = jnp.where(
                    keep, tile, jnp.zeros_like(tile)
                )
        sums = jnp.dot(
            placed[:, pl.ds(step * per_step * edge, per_step * edge)], ones, preferred_element_type=F32
        )
        if step == 0:
            degree[...] = sums
        else:
            degree[...] += sums

    steps = slots // per_step

    def first_work(s):
        if s == 0:
            weights[core, 0] = self_weight[0]
            weights[core, 1] = neighbor_weight[0]
            hidden.append(send(weights.at[core], weights.at[core], device(dc=1)))
            tile_copy.wait()
        if half_z >= 8:
            if 1 <= s <= steps:
                place(s - 1)
            final = s == steps + 1
        else:
            if s == 0:
                for step in range(steps):
                    place(step)
            final = s == 1
        if final:
            for j in range(1, reps):
                hidden.append(
                    send(degree.at[pl.ds(j * edge, edge)], degree_arrived.at[j - 1], device(dr=j))
                )
        if s == half_z:
            hidden[0].wait_recv()
            own_product[...] = jnp.dot(nodes[0], weights[0, 0], preferred_element_type=F32)

    def second_work(s):
        if s == 1:
            own_product[...] = jnp.dot(nodes[1], weights[1, 0], preferred_element_type=F32)

    def aggregate(layer):
        a, b = parts_a[layer], parts_b[layer]
        for k in range(slots):
            d = (section[0, 0, k] // RING_Y - z + ring_z) % ring_z
            e = (section[0, 0, k] % RING_Y - y + RING_Y) % RING_Y
            at = jnp.where(
                d < half_z, 2 * d, jnp.where(d == half_z, ring_z - 1, 2 * (ring_z - d) - 1)
            )
            panels[pl.ds(k * edge, rows_a), :] = a[at * RING_Y + e]
            panels[pl.ds(k * edge + rows_a, rows_b), :] = b[e, at]
        copies = []
        for j in [reps // 2] + [j for j in range(1, reps) if j != reps // 2] + [0]:
            total = jnp.dot(
                placed[pl.ds(j * edge, edge), :], panels[...], preferred_element_type=F32
            ).astype(BF16)
            if j == 0:
                arrived[layer, 0, core] = total
            else:
                to_send[layer, j - 1] = total
            if layer == 0:
                if j > 0:
                    source = to_send.at[layer, j - 1]
                    copies.append(send(source, arrived.at[layer, j, core], device(dr=j)))
                else:
                    source = arrived.at[layer, 0, core]
                copies.append(
                    send(source, arrived.at[layer, j, core], device(dr=j, dc=1))
                )
            elif j > 0:
                copies.append(to_second(j))
                copies[-1].start()
        return copies

    def to_second(j, from_core=None):
        from_core = core if from_core is None else from_core
        at = len(started_slots) + 2 * (j - 1)
        return pltpu.make_async_remote_copy(
            src_ref=to_send.at[1, j - 1],
            dst_ref=arrived.at[1, j, from_core],
            send_sem=send_sem.at[at],
            recv_sem=recv_sem.at[at + from_core],
            device_id=(1,) + device(dr=j)[1:],
            device_id_type=MESH,
        )

    def mixture(layer, scale):
        z_sum = own_product[...]
        for c in range(2):
            near = sum(arrived[layer, j, c].astype(F32) for j in range(reps))
            agg = (near * scale).astype(BF16)
            z_sum = z_sum + jnp.dot(
                agg, weights[layer, 1, c * half_f : (c + 1) * half_f, :], preferred_element_type=F32
            )
        return z_sum

    gather(0, inputs, first_work)
    copies = aggregate(0)
    for copy in hidden[1:] + copies:
        copy.wait_recv()
    total_degree = degree[:edge, :]
    for j in range(1, reps):
        total_degree = total_degree + degree_arrived[j - 1]
    degree[:edge, :] = lax.rsqrt(total_degree)
    active = jnp.maximum(mixture(0, degree[:edge, :]), 0.0)
    center = active - jnp.mean(active, axis=-1, keepdims=True)
    spread = jnp.mean(center * center, axis=-1, keepdims=True)
    first = (center * lax.rsqrt(spread + 1e-05) * norm_scale[...]).astype(BF16)
    nodes[1] = first

    gather(1, first, second_work)
    started_slots = list(started)
    copies = aggregate(1)
    last_at = len(started_slots) + 2 * (reps - 1)
    across = pltpu.make_async_remote_copy(
        src_ref=arrived.at[1, 0, 0],
        dst_ref=arrived.at[1, 0, 0],
        send_sem=send_sem.at[last_at],
        recv_sem=recv_sem.at[last_at],
        device_id=(1, row, rep),
        device_id_type=MESH,
    )

    @pl.when(core == 0)
    def _():
        across.start()
        out[0] = nodes[1]
        across.wait_send()

    @pl.when(core == 1)
    def _():
        for j in range(1, reps):
            for c in range(2):
                to_second(j, c).wait_recv()
        across.wait_recv()
        out[0] = mixture(1, degree[:edge, :]).astype(BF16)

    for copy in started_slots + copies:
        copy.wait_send()


def solution(mesh):
    reps = mesh.shape["rep"]
    ring_z = mesh.shape["row"] // RING_Y

    def body(
        features,
        class_ids,
        label_table,
        self_weight,
        neighbor_weight,
        norm_scale,
        tile_values,
        block_row,
        section,
        count,
    ):
        slots, edge = tile_values.shape[2:4]
        width = features.shape[1]
        half = width // 2
        rows_b = edge - ROWS_A
        vmem = pl.BlockSpec(memory_space=pltpu.VMEM)
        smem = pl.BlockSpec(memory_space=pltpu.SMEM)
        copies = 2 * (3 + 6 * ring_z) + 8 * reps + 16
        return pl.pallas_call(
            functools.partial(kernel, ring_z, reps),
            out_shape=jax.ShapeDtypeStruct((1, edge, width), BF16),
            in_specs=[vmem] * 6 + [pl.BlockSpec(memory_space=pl.ANY)] + [smem] * 3,
            out_specs=vmem,
            scratch_shapes=[
                pltpu.VMEM((slots, edge, edge), BF16),
                pltpu.VMEM((reps * edge, slots * edge), BF16),
                pltpu.VMEM((slots * edge, half), BF16),
                pltpu.VMEM((ring_z * RING_Y, ROWS_A, half), BF16),
                pltpu.VMEM((RING_Y, ring_z, rows_b, half), BF16),
                pltpu.VMEM((ring_z * RING_Y, ROWS_A, half), BF16),
                pltpu.VMEM((RING_Y, ring_z, rows_b, half), BF16),
                pltpu.VMEM((2, 2, width, width), BF16),
                pltpu.VMEM((2, edge, width), BF16),
                pltpu.VMEM((edge, width), F32),
                pltpu.VMEM((2, reps - 1, edge, half), BF16),
                pltpu.VMEM((2, reps, 2, edge, half), BF16),
                pltpu.VMEM((reps * edge, half), F32),
                pltpu.VMEM((reps - 1, edge, half), F32),
                pltpu.SemaphoreType.DMA((copies,)),
                pltpu.SemaphoreType.DMA((copies,)),
                pltpu.SemaphoreType.DMA,
            ],
            compiler_params=pltpu.CompilerParams(
                collective_id=0, has_side_effects=True, vmem_limit_bytes=40 * 2**20
            ),
        )(
            features,
            class_ids.reshape(1, edge),
            label_table,
            self_weight,
            neighbor_weight,
            norm_scale.reshape(1, width),
            tile_values,
            block_row,
            section,
            count,
        )

    return jax.shard_map(
        body,
        mesh=mesh,
        in_specs=(
            P(("row", "rep"), None),
            P(("row", "rep")),
            P(),
            P("layer", None, None),
            P("layer", None, None),
            P(),
            P("row", "rep", None, None, None),
            P("row", "rep", None),
            P("row", "rep", None),
            P("row", "rep"),
        ),
        out_specs=P("layer", ("row", "rep"), None),
        check_vma=False,
    )
```

```python
import functools

import jax
import jax.numpy as jnp
from jax import lax
from jax.experimental import pallas as pl
from jax.experimental.pallas import tpu as pltpu
from jax.sharding import PartitionSpec as P

MESH = pl.DeviceIdType.MESH
RING_Y = 4
ROWS_A = 64
STRIDE = 3
F32 = jnp.float32
BF16 = jnp.bfloat16


def kernel(
    ring_z,
    reps,
    features_in,
    class_ids_in,
    label_table_in,
    self_weight,
    neighbor_weight,
    norm_scale_in,
    tile_values,
    block_row_in,
    section_in,
    count_in,
    out,
    features,
    class_ids,
    label_table,
    norm_scale,
    block_row,
    section,
    count,
    tiles,
    placed,
    panels,
    first_a,
    first_b,
    second_a,
    second_b,
    weights,
    nodes,
    own_product,
    to_send,
    arrived,
    degree,
    degree_arrived,
    send_sem,
    recv_sem,
    load_sem,
):
    slots = tiles.shape[0]
    edge = tiles.shape[1]
    parts_a, parts_b = (first_a, second_a), (first_b, second_b)
    rows_a, half_f = first_a.shape[1:]
    rows_b = first_b.shape[2]
    half_z = ring_z // 2
    core = lax.axis_index("layer")
    row = lax.axis_index("row")
    rep = lax.axis_index("rep")
    z, y = row // RING_Y, row % RING_Y

    def device(dz=0, dy=0, dr=0, dc=0):
        to_row = ((z + dz + ring_z) % ring_z) * RING_Y + (y + dy + RING_Y) % RING_Y
        return ((core + dc) % 2, to_row, (rep + dr) % reps)

    def z_slot(d):
        return (d + half_z - 1) % ring_z

    started = []

    def send(src, dst, device_id):
        at = len(started)
        copy = pltpu.make_async_remote_copy(
            src_ref=src,
            dst_ref=dst,
            send_sem=send_sem.at[at],
            recv_sem=recv_sem.at[at],
            device_id=device_id,
            device_id_type=MESH,
        )
        copy.start()
        started.append(copy)
        return copy

    loads = [
        pltpu.make_async_copy(src, dst, load_sem.at[i])
        for i, (src, dst) in enumerate(
            [
                (class_ids_in, class_ids),
                (label_table_in, label_table),
                (features_in, features),
                (block_row_in, block_row),
                (section_in, section),
                (count_in, count),
                (norm_scale_in, norm_scale),
                (tile_values.at[0, 0], tiles),
                (self_weight.at[0], weights.at[core, 0]),
                (neighbor_weight.at[0], weights.at[core, 1]),
            ]
        )
    ]
    for load in loads:
        load.start()

    barrier = pltpu.get_barrier_semaphore()
    friends = [device(dz=d) for d in (1, -1, 2, -2, STRIDE, -STRIDE)]
    friends += [device(dy=1), device(dy=-1), device(dy=2), device(dc=1)]
    for j in range(1, reps):
        friends += [device(dr=j), device(dr=j, dc=1)]
    for friend in friends:
        pl.semaphore_signal(barrier, inc=1, device_id=friend, device_id_type=MESH)

    for load in loads[:3]:
        load.wait()
    classes = label_table.shape[0]
    one_hot = (
        lax.broadcasted_iota(jnp.int32, (classes, edge), 0) == class_ids[...]
    ).astype(F32).astype(BF16)
    labels = lax.dot_general(
        one_hot, label_table[...], (((0,), (0,)), ((), ())), preferred_element_type=F32
    )
    inputs = (features[...].astype(F32) + labels).astype(BF16)
    nodes[0] = inputs

    def own_half(whole):
        return jnp.where(core == 0, whole[:, :half_f].astype(F32), whole[:, half_f:].astype(F32)).astype(BF16)

    def gather(layer, whole, work):
        a, b = parts_a[layer], parts_b[layer]
        mine = own_half(whole)
        a[z_slot(0) * RING_Y] = mine[:rows_a]
        b[0, z_slot(0)] = mine[rows_a:]
        if layer == 0:
            pl.semaphore_wait(barrier, len(friends))

        def along_y(src_of, dst_of):
            return [
                send(src_of, dst_of((RING_Y - dy) % RING_Y), device(dy=dy)) for dy in (2, 1, -1)
            ]

        def block(d):
            return a.at[pl.ds(z_slot(d) * RING_Y, RING_Y)]

        def chain(d, up):
            to = d - STRIDE if up else d + STRIDE
            target = device(dz=STRIDE if up else -STRIDE)
            return [
                send(
                    a.at[z_slot(d) * RING_Y],
                    a.at[z_slot(to) * RING_Y],
                    target,
                ),
                send(b.at[0, z_slot(d)], b.at[0, z_slot(to)], target),
            ]

        def a_spread(d):
            at = z_slot(d) * RING_Y
            return along_y(a.at[at], lambda e: a.at[at + e])

        def a_local(d):
            return [
                send(block(d), block(d - 1), device(dz=1)),
                send(block(d), block(d + 1), device(dz=-1)),
            ]

        def b_local(d):
            at = z_slot(d)
            return [
                send(b.at[0, at], b.at[0, at - 1], device(dz=1)),
                send(b.at[0, at], b.at[0, at + 1], device(dz=-1)),
            ]

        def b_spread(d, many=3):
            at = pl.ds(z_slot(d) - many // 2, many)
            return along_y(b.at[0, at], lambda e: b.at[e, at])

        def wait(copies):
            for copy in copies:
                copy.wait_recv()

        steps = (ring_z - 1) // STRIDE // 2
        last = []
        relays = [0]
        for step in range(steps + 1):
            ahead = []
            if step < steps:
                ahead = chain(relays[0], True) + chain(relays[-1], False)
            near, side = [], []
            for d in relays:
                near += b_local(d)
                side += a_spread(d)
            if step == steps:
                near.append(
                    send(
                        b.at[0, z_slot(relays[0])],
                        b.at[0, ring_z - 1],
                        device(dz=2),
                    )
                )
            work(2 * step)
            wait(near[: 2 * len(relays)])
            for d in relays:
                last += b_spread(d)
            wait(side)
            for d in relays:
                last += a_local(d)
            if step == steps:
                last.append(send(block(relays[-1]), block(half_z), device(dz=-2)))
                wait(near[2 * len(relays) :])
                last += b_spread(half_z, 1)
            work(2 * step + 1)
            wait(ahead)
            relays = [-STRIDE * (step + 1), STRIDE * (step + 1)]
        wait(last)

    for load in loads[3:]:
        load.wait()
    filled = count[0, 0]
    targets = [(block_row[0, 0, k] - rep + reps) % reps for k in range(slots)]
    per_step = max(slots // 4, 1)
    ones = jnp.ones((per_step * edge, half_f), BF16)
    hidden = []

    def place(step):
        for k in range(step * per_step, (step + 1) * per_step):
            tile = tiles[k]
            for j in range(reps):
                keep = jnp.logical_and(targets[k] == j, k < filled)
                placed[pl.ds(j * edge, edge), pl.ds(k * edge, edge)] = jnp.where(
                    keep, tile, jnp.zeros_like(tile)
                )
        sums = jnp.dot(
            placed[:, pl.ds(step * per_step * edge, per_step * edge)], ones, preferred_element_type=F32
        )
        if step == 0:
            degree[...] = sums
        else:
            degree[...] += sums

    pieces = slots // per_step

    def first_work(at):
        if at == 0:
            hidden.append(send(weights.at[core], weights.at[core], device(dc=1)))
            for piece in range(pieces // 2):
                place(piece)
        if at == 1:
            for piece in range(pieces // 2, pieces):
                place(piece)
            for j in range(1, reps):
                hidden.append(
                    send(degree.at[pl.ds(j * edge, edge)], degree_arrived.at[j - 1], device(dr=j))
                )
            hidden[0].wait_recv()
            own_product[...] = jnp.dot(nodes[0], weights[0, 0], preferred_element_type=F32)

    def second_work(s):
        if s == 1:
            own_product[...] = jnp.dot(nodes[1], weights[1, 0], preferred_element_type=F32)

    def aggregate(layer):
        a, b = parts_a[layer], parts_b[layer]
        for k in range(slots):
            at = (section[0, 0, k] // RING_Y - z + ring_z + half_z - 1) % ring_z
            e = (section[0, 0, k] % RING_Y - y + RING_Y) % RING_Y
            panels[pl.ds(k * edge, rows_a), :] = a[at * RING_Y + e]
            panels[pl.ds(k * edge + rows_a, rows_b), :] = b[e, at]
        copies = []
        for j in [reps // 2] + [j for j in range(1, reps) if j != reps // 2] + [0]:
            total = jnp.dot(
                placed[pl.ds(j * edge, edge), :], panels[...], preferred_element_type=F32
            ).astype(BF16)
            if j == 0:
                arrived[layer, 0, core] = total
            else:
                to_send[layer, j - 1] = total
            if layer == 0:
                if j > 0:
                    source = to_send.at[layer, j - 1]
                    copies.append(send(source, arrived.at[layer, j, core], device(dr=j)))
                else:
                    source = arrived.at[layer, 0, core]
                copies.append(
                    send(source, arrived.at[layer, j, core], device(dr=j, dc=1))
                )
            elif j > 0:
                copies.append(to_second(j))
                copies[-1].start()
        return copies

    def to_second(j, from_core=None):
        from_core = core if from_core is None else from_core
        at = len(started_slots) + 2 * (j - 1)
        return pltpu.make_async_remote_copy(
            src_ref=to_send.at[1, j - 1],
            dst_ref=arrived.at[1, j, from_core],
            send_sem=send_sem.at[at],
            recv_sem=recv_sem.at[at + from_core],
            device_id=(1,) + device(dr=j)[1:],
            device_id_type=MESH,
        )

    def mixture(layer, scale):
        z_sum = own_product[...]
        for c in range(2):
            near = sum(arrived[layer, j, c].astype(F32) for j in range(reps))
            agg = (near * scale).astype(BF16)
            z_sum = z_sum + jnp.dot(
                agg, weights[layer, 1, c * half_f : (c + 1) * half_f, :], preferred_element_type=F32
            )
        return z_sum

    gather(0, inputs, first_work)
    copies = aggregate(0)
    for copy in hidden[1:] + copies:
        copy.wait_recv()
    total_degree = degree[:edge, :]
    for j in range(1, reps):
        total_degree = total_degree + degree_arrived[j - 1]
    degree[:edge, :] = lax.rsqrt(total_degree)
    active = jnp.maximum(mixture(0, degree[:edge, :]), 0.0)
    center = active - jnp.mean(active, axis=-1, keepdims=True)
    spread = jnp.mean(center * center, axis=-1, keepdims=True)
    first = (center * lax.rsqrt(spread + 1e-05) * norm_scale[...]).astype(BF16)
    nodes[1] = first

    gather(1, first, second_work)
    started_slots = list(started)
    copies = aggregate(1)
    last_at = len(started_slots) + 2 * (reps - 1)
    across = pltpu.make_async_remote_copy(
        src_ref=arrived.at[1, 0, 0],
        dst_ref=arrived.at[1, 0, 0],
        send_sem=send_sem.at[last_at],
        recv_sem=recv_sem.at[last_at],
        device_id=(1, row, rep),
        device_id_type=MESH,
    )

    @pl.when(core == 0)
    def _():
        across.start()
        out[0] = nodes[1]
        across.wait_send()

    @pl.when(core == 1)
    def _():
        for j in range(1, reps):
            for c in range(2):
                to_second(j, c).wait_recv()
        across.wait_recv()
        out[0] = mixture(1, degree[:edge, :]).astype(BF16)

    for copy in started_slots + copies:
        copy.wait_send()


def solution(mesh):
    reps = mesh.shape["rep"]
    ring_z = mesh.shape["row"] // RING_Y

    def body(
        features,
        class_ids,
        label_table,
        self_weight,
        neighbor_weight,
        norm_scale,
        tile_values,
        block_row,
        section,
        count,
    ):
        slots, edge = tile_values.shape[2:4]
        width = features.shape[1]
        half = width // 2
        rows_b = edge - ROWS_A
        vmem = pl.BlockSpec(memory_space=pltpu.VMEM)
        hbm = pl.BlockSpec(memory_space=pltpu.HBM)
        classes = label_table.shape[0]
        copies = 2 * (3 + 6 * ring_z) + 8 * reps + 16
        return pl.pallas_call(
            functools.partial(kernel, ring_z, reps),
            out_shape=jax.ShapeDtypeStruct((1, edge, width), BF16),
            in_specs=[hbm] * 10,
            out_specs=vmem,
            scratch_shapes=[
                pltpu.VMEM((edge, width), BF16),
                pltpu.VMEM((1, edge), jnp.int32),
                pltpu.VMEM((classes, width), BF16),
                pltpu.VMEM((1, width), F32),
                pltpu.SMEM((1, 1, slots), jnp.int32),
                pltpu.SMEM((1, 1, slots), jnp.int32),
                pltpu.SMEM((1, 1), jnp.int32),
                pltpu.VMEM((slots, edge, edge), BF16),
                pltpu.VMEM((reps * edge, slots * edge), BF16),
                pltpu.VMEM((slots * edge, half), BF16),
                pltpu.VMEM((ring_z * RING_Y, ROWS_A, half), BF16),
                pltpu.VMEM((RING_Y, ring_z, rows_b, half), BF16),
                pltpu.VMEM((ring_z * RING_Y, ROWS_A, half), BF16),
                pltpu.VMEM((RING_Y, ring_z, rows_b, half), BF16),
                pltpu.VMEM((2, 2, width, width), BF16),
                pltpu.VMEM((2, edge, width), BF16),
                pltpu.VMEM((edge, width), F32),
                pltpu.VMEM((2, reps - 1, edge, half), BF16),
                pltpu.VMEM((2, reps, 2, edge, half), BF16),
                pltpu.VMEM((reps * edge, half), F32),
                pltpu.VMEM((reps - 1, edge, half), F32),
                pltpu.SemaphoreType.DMA((copies,)),
                pltpu.SemaphoreType.DMA((copies,)),
                pltpu.SemaphoreType.DMA((10,)),
            ],
            compiler_params=pltpu.CompilerParams(
                collective_id=0, has_side_effects=True, vmem_limit_bytes=64 * 2**20
            ),
        )(
            features,
            class_ids.reshape(1, edge),
            label_table,
            self_weight,
            neighbor_weight,
            norm_scale.reshape(1, width),
            tile_values,
            block_row,
            section,
            count,
        )

    return jax.shard_map(
        body,
        mesh=mesh,
        in_specs=(
            P(("row", "rep"), None),
            P(("row", "rep")),
            P(),
            P("layer", None, None),
            P("layer", None, None),
            P(),
            P("row", "rep", None, None, None),
            P("row", "rep", None),
            P("row", "rep", None),
            P("row", "rep"),
        ),
        out_specs=P("layer", ("row", "rep"), None),
        check_vma=False,
    )
```

```python
import functools

import jax
import jax.numpy as jnp
from jax import lax
from jax.experimental import pallas as pl
from jax.experimental.pallas import tpu as pltpu
from jax.sharding import PartitionSpec as P

MESH = pl.DeviceIdType.MESH
RING_Y = 4
ROWS_A = 64
RELAYS = [(-3, 0), (3, 0), (-6, -3), (6, 3)]
LOCALS = [1, -1]
FAR_FROM = -6
F32 = jnp.float32
BF16 = jnp.bfloat16


def far_step(ring_z):
    return ring_z // 2 + FAR_FROM if ring_z > 4 else 2


def kernel(
    ring_z,
    reps,
    features_in,
    class_ids_in,
    label_table_in,
    self_weight,
    neighbor_weight,
    norm_scale_in,
    tile_values,
    block_row_in,
    section_in,
    count_in,
    out,
    features,
    class_ids,
    label_table,
    norm_scale,
    block_row,
    section,
    count,
    tiles,
    placed,
    panels,
    first_chunks,
    second_chunks,
    weights,
    nodes,
    own_product,
    to_send,
    arrived,
    degree,
    degree_arrived,
    send_sem,
    recv_sem,
    load_sem,
):
    slots = tiles.shape[0]
    edge = tiles.shape[1]
    chunks = (first_chunks, second_chunks)
    half_f = first_chunks.shape[-1]
    half_z = ring_z // 2
    core = lax.axis_index("layer")
    row = lax.axis_index("row")
    rep = lax.axis_index("rep")
    z, y = row // RING_Y, row % RING_Y

    def device(dz=0, dy=0, dr=0, dc=0):
        to_row = ((z + dz + ring_z) % ring_z) * RING_Y + (y + dy + RING_Y) % RING_Y
        return ((core + dc) % 2, to_row, (rep + dr) % reps)

    def z_slot(d):
        return (d + half_z - 1) % ring_z

    started = []

    def send(src, dst, device_id):
        at = len(started)
        copy = pltpu.make_async_remote_copy(
            src_ref=src,
            dst_ref=dst,
            send_sem=send_sem.at[at],
            recv_sem=recv_sem.at[at],
            device_id=device_id,
            device_id_type=MESH,
        )
        copy.start()
        started.append(copy)
        return copy

    loads = [
        pltpu.make_async_copy(src, dst, load_sem.at[i])
        for i, (src, dst) in enumerate(
            [
                (class_ids_in, class_ids),
                (label_table_in, label_table),
                (features_in, features),
                (block_row_in, block_row),
                (section_in, section),
                (count_in, count),
                (norm_scale_in, norm_scale),
                (tile_values.at[0, 0], tiles),
                (self_weight.at[0], weights.at[core, 0]),
                (neighbor_weight.at[0], weights.at[core, 1]),
            ]
        )
    ]
    for load in loads:
        load.start()

    barrier = pltpu.get_barrier_semaphore()
    relays = RELAYS if ring_z > 4 else []
    steps_z = set(LOCALS) | {d - parent for d, parent in relays}
    steps_z |= {-d for d in steps_z} | {far_step(ring_z), -far_step(ring_z)}
    friends = [device(dz=d) for d in sorted(steps_z)]
    friends += [device(dy=1), device(dy=-1), device(dy=2), device(dc=1)]
    for j in range(1, reps):
        friends += [device(dr=j), device(dr=j, dc=1)]
    for friend in friends:
        pl.semaphore_signal(barrier, inc=1, device_id=friend, device_id_type=MESH)

    for load in loads[:3]:
        load.wait()
    classes = label_table.shape[0]
    one_hot = (
        lax.broadcasted_iota(jnp.int32, (classes, edge), 0) == class_ids[...]
    ).astype(F32).astype(BF16)
    labels = lax.dot_general(
        one_hot, label_table[...], (((0,), (0,)), ((), ())), preferred_element_type=F32
    )
    inputs = (features[...].astype(F32) + labels).astype(BF16)
    nodes[0] = inputs

    def own_half(whole):
        return jnp.where(core == 0, whole[:, :half_f].astype(F32), whole[:, half_f:].astype(F32)).astype(BF16)

    def gather(layer, whole, work):
        held = chunks[layer]
        top, bottom = slice(0, ROWS_A), slice(ROWS_A, None)
        held[z_slot(0) * RING_Y] = own_half(whole)
        if layer == 0:
            pl.semaphore_wait(barrier, len(friends))

        def at(d, e=0):
            return z_slot(d) * RING_Y + e % RING_Y

        def relay(d, to):
            return send(held.at[at(d)], held.at[at(to)], device(dz=d - to))

        def along_y(d, rows=slice(None)):
            return [
                send(held.at[at(d), rows], held.at[at(d, -dy), rows], device(dy=dy))
                for dy in (2, 1, -1)
            ]

        def spread(d):
            onward = [(to, relay(d, to)) for to, parent in relays if parent == d]
            near = [
                (dz, send(held.at[at(d)], held.at[at(d - dz)], device(dz=dz))) for dz in LOCALS
            ]
            side = along_y(d)
            across = []
            if d == (FAR_FROM if relays else 0):
                across = [
                    send(held.at[at(d)], held.at[at(half_z)], device(dz=far_step(ring_z)))
                ]
            return onward, near, side, across

        last = []

        def corners(d, near, side):
            for dz, copy in near:
                copy.wait_recv()
                last.extend(along_y(d - dz, bottom))
            for copy in side:
                copy.wait_recv()
            for dz in LOCALS:
                last.append(
                    send(
                        held.at[pl.ds(at(d, 1), RING_Y - 1), top],
                        held.at[pl.ds(at(d - dz, 1), RING_Y - 1), top],
                        device(dz=dz),
                    )
                )

        coming, near, side, opposite = spread(0)
        work(0)
        corners(0, near, side)
        work(1)
        pending = []
        while coming:
            d, copy = coming.pop(0)
            copy.wait_recv()
            onward, near, side, across = spread(d)
            coming += onward
            opposite += across
            pending.append((d, near, side))
        for entry in pending:
            corners(*entry)
        opposite[0].wait_recv()
        last.extend(along_y(half_z))
        for copy in last:
            copy.wait_recv()

    for load in loads[3:]:
        load.wait()
    filled = count[0, 0]
    targets = [(block_row[0, 0, k] - rep + reps) % reps for k in range(slots)]
    per_step = max(slots // 4, 1)
    ones = jnp.ones((per_step * edge, half_f), BF16)
    hidden = []

    def place(step):
        for k in range(step * per_step, (step + 1) * per_step):
            tile = tiles[k]
            for j in range(reps):
                keep = jnp.logical_and(targets[k] == j, k < filled)
                placed[pl.ds(j * edge, edge), pl.ds(k * edge, edge)] = jnp.where(
                    keep, tile, jnp.zeros_like(tile)
                )
        sums = jnp.dot(
            placed[:, pl.ds(step * per_step * edge, per_step * edge)], ones, preferred_element_type=F32
        )
        if step == 0:
            degree[...] = sums
        else:
            degree[...] += sums

    pieces = slots // per_step

    def first_work(at):
        if at == 0:
            hidden.append(send(weights.at[core], weights.at[core], device(dc=1)))
            for piece in range(pieces // 2):
                place(piece)
        if at == 1:
            for piece in range(pieces // 2, pieces):
                place(piece)
            for j in range(1, reps):
                hidden.append(
                    send(degree.at[pl.ds(j * edge, edge)], degree_arrived.at[j - 1], device(dr=j))
                )
            hidden[0].wait_recv()
            own_product[...] = jnp.dot(nodes[0], weights[0, 0], preferred_element_type=F32)

    def second_work(s):
        if s == 1:
            own_product[...] = jnp.dot(nodes[1], weights[1, 0], preferred_element_type=F32)

    def aggregate(layer):
        held = chunks[layer]
        for k in range(slots):
            at = (section[0, 0, k] // RING_Y - z + ring_z + half_z - 1) % ring_z
            e = (section[0, 0, k] % RING_Y - y + RING_Y) % RING_Y
            panels[pl.ds(k * edge, edge), :] = held[at * RING_Y + e]
        copies = []
        for j in [reps // 2] + [j for j in range(1, reps) if j != reps // 2] + [0]:
            total = jnp.dot(
                placed[pl.ds(j * edge, edge), :], panels[...], preferred_element_type=F32
            ).astype(BF16)
            if j == 0:
                arrived[layer, 0, core] = total
            else:
                to_send[layer, j - 1] = total
            if layer == 0:
                if j > 0:
                    source = to_send.at[layer, j - 1]
                    copies.append(send(source, arrived.at[layer, j, core], device(dr=j)))
                else:
                    source = arrived.at[layer, 0, core]
                copies.append(
                    send(source, arrived.at[layer, j, core], device(dr=j, dc=1))
                )
            elif j > 0:
                copies.append(to_second(j))
                copies[-1].start()
        return copies

    def to_second(j, from_core=None):
        from_core = core if from_core is None else from_core
        at = len(started_slots) + 2 * (j - 1)
        return pltpu.make_async_remote_copy(
            src_ref=to_send.at[1, j - 1],
            dst_ref=arrived.at[1, j, from_core],
            send_sem=send_sem.at[at],
            recv_sem=recv_sem.at[at + from_core],
            device_id=(1,) + device(dr=j)[1:],
            device_id_type=MESH,
        )

    def mixture(layer, scale):
        z_sum = own_product[...]
        for c in range(2):
            near = sum(arrived[layer, j, c].astype(F32) for j in range(reps))
            agg = (near * scale).astype(BF16)
            z_sum = z_sum + jnp.dot(
                agg, weights[layer, 1, c * half_f : (c + 1) * half_f, :], preferred_element_type=F32
            )
        return z_sum

    gather(0, inputs, first_work)
    copies = aggregate(0)
    for copy in hidden[1:] + copies:
        copy.wait_recv()
    total_degree = degree[:edge, :]
    for j in range(1, reps):
        total_degree = total_degree + degree_arrived[j - 1]
    degree[:edge, :] = lax.rsqrt(total_degree)
    active = jnp.maximum(mixture(0, degree[:edge, :]), 0.0)
    center = active - jnp.mean(active, axis=-1, keepdims=True)
    spread = jnp.mean(center * center, axis=-1, keepdims=True)
    first = (center * lax.rsqrt(spread + 1e-05) * norm_scale[...]).astype(BF16)
    nodes[1] = first

    gather(1, first, second_work)
    started_slots = list(started)
    copies = aggregate(1)
    last_at = len(started_slots) + 2 * (reps - 1)
    across = pltpu.make_async_remote_copy(
        src_ref=arrived.at[1, 0, 0],
        dst_ref=arrived.at[1, 0, 0],
        send_sem=send_sem.at[last_at],
        recv_sem=recv_sem.at[last_at],
        device_id=(1, row, rep),
        device_id_type=MESH,
    )

    @pl.when(core == 0)
    def _():
        across.start()
        out[0] = nodes[1]
        across.wait_send()

    @pl.when(core == 1)
    def _():
        for j in range(1, reps):
            for c in range(2):
                to_second(j, c).wait_recv()
        across.wait_recv()
        out[0] = mixture(1, degree[:edge, :]).astype(BF16)

    for copy in started_slots + copies:
        copy.wait_send()


def solution(mesh):
    reps = mesh.shape["rep"]
    ring_z = mesh.shape["row"] // RING_Y

    def body(
        features,
        class_ids,
        label_table,
        self_weight,
        neighbor_weight,
        norm_scale,
        tile_values,
        block_row,
        section,
        count,
    ):
        slots, edge = tile_values.shape[2:4]
        width = features.shape[1]
        half = width // 2
        vmem = pl.BlockSpec(memory_space=pltpu.VMEM)
        hbm = pl.BlockSpec(memory_space=pltpu.HBM)
        classes = label_table.shape[0]
        copies = 2 * (3 + 6 * ring_z) + 8 * reps + 16
        return pl.pallas_call(
            functools.partial(kernel, ring_z, reps),
            out_shape=jax.ShapeDtypeStruct((1, edge, width), BF16),
            in_specs=[hbm] * 10,
            out_specs=vmem,
            scratch_shapes=[
                pltpu.VMEM((edge, width), BF16),
                pltpu.VMEM((1, edge), jnp.int32),
                pltpu.VMEM((classes, width), BF16),
                pltpu.VMEM((1, width), F32),
                pltpu.SMEM((1, 1, slots), jnp.int32),
                pltpu.SMEM((1, 1, slots), jnp.int32),
                pltpu.SMEM((1, 1), jnp.int32),
                pltpu.VMEM((slots, edge, edge), BF16),
                pltpu.VMEM((reps * edge, slots * edge), BF16),
                pltpu.VMEM((slots * edge, half), BF16),
                pltpu.VMEM((ring_z * RING_Y, edge, half), BF16),
                pltpu.VMEM((ring_z * RING_Y, edge, half), BF16),
                pltpu.VMEM((2, 2, width, width), BF16),
                pltpu.VMEM((2, edge, width), BF16),
                pltpu.VMEM((edge, width), F32),
                pltpu.VMEM((2, reps - 1, edge, half), BF16),
                pltpu.VMEM((2, reps, 2, edge, half), BF16),
                pltpu.VMEM((reps * edge, half), F32),
                pltpu.VMEM((reps - 1, edge, half), F32),
                pltpu.SemaphoreType.DMA((copies,)),
                pltpu.SemaphoreType.DMA((copies,)),
                pltpu.SemaphoreType.DMA((10,)),
            ],
            compiler_params=pltpu.CompilerParams(
                collective_id=0, has_side_effects=True, vmem_limit_bytes=64 * 2**20
            ),
        )(
            features,
            class_ids.reshape(1, edge),
            label_table,
            self_weight,
            neighbor_weight,
            norm_scale.reshape(1, width),
            tile_values,
            block_row,
            section,
            count,
        )

    return jax.shard_map(
        body,
        mesh=mesh,
        in_specs=(
            P(("row", "rep"), None),
            P(("row", "rep")),
            P(),
            P("layer", None, None),
            P("layer", None, None),
            P(),
            P("row", "rep", None, None, None),
            P("row", "rep", None),
            P("row", "rep", None),
            P("row", "rep"),
        ),
        out_specs=P("layer", ("row", "rep"), None),
        check_vma=False,
    )
```

```python
import functools

import jax
import jax.numpy as jnp
from jax import lax
from jax.experimental import pallas as pl
from jax.experimental.pallas import tpu as pltpu
from jax.sharding import PartitionSpec as P

MESH = pl.DeviceIdType.MESH
RING_Y = 4
ROWS_A = 64
RELAYS = [(-3, 0), (3, 0), (-6, -3), (6, 3)]
LOCALS = [1, -1]
FAR_FROM = -6
F32 = jnp.float32
BF16 = jnp.bfloat16


def far_step(ring_z):
    return ring_z // 2 + FAR_FROM if ring_z > 4 else 2


def kernel(
    ring_z,
    reps,
    features_in,
    class_ids_in,
    label_table_in,
    self_weight,
    neighbor_weight,
    norm_scale_in,
    tile_values,
    block_row_in,
    section_in,
    count_in,
    out,
    features,
    class_ids,
    label_table,
    norm_scale,
    block_row,
    section,
    count,
    tiles,
    placed,
    panels,
    first_chunks,
    second_chunks,
    weights,
    nodes,
    own_product,
    to_send,
    arrived,
    degree,
    degree_arrived,
    send_sem,
    recv_sem,
    load_sem,
):
    slots = tiles.shape[0]
    edge = tiles.shape[1]
    chunks = (first_chunks, second_chunks)
    half_f = first_chunks.shape[-1]
    half_z = ring_z // 2
    core = lax.axis_index("layer")
    row = lax.axis_index("row")
    rep = lax.axis_index("rep")
    z, y = row // RING_Y, row % RING_Y

    def device(dz=0, dy=0, dr=0, dc=0):
        to_row = ((z + dz + ring_z) % ring_z) * RING_Y + (y + dy + RING_Y) % RING_Y
        return ((core + dc) % 2, to_row, (rep + dr) % reps)

    def z_slot(d):
        return (d + half_z - 1) % ring_z

    started = []

    def send(src, dst, device_id):
        at = len(started)
        copy = pltpu.make_async_remote_copy(
            src_ref=src,
            dst_ref=dst,
            send_sem=send_sem.at[at],
            recv_sem=recv_sem.at[at],
            device_id=device_id,
            device_id_type=MESH,
        )
        copy.start()
        started.append(copy)
        return copy

    loads = [
        pltpu.make_async_copy(src, dst, load_sem.at[i])
        for i, (src, dst) in enumerate(
            [
                (class_ids_in, class_ids),
                (label_table_in, label_table),
                (features_in, features),
                (block_row_in, block_row),
                (section_in, section),
                (count_in, count),
                (norm_scale_in, norm_scale),
                (tile_values.at[0, 0], tiles),
                (self_weight.at[0], weights.at[core, 0]),
                (neighbor_weight.at[0], weights.at[core, 1]),
            ]
        )
    ]
    for load in loads:
        load.start()

    barrier = pltpu.get_barrier_semaphore()
    relays = RELAYS if ring_z > 4 else []
    steps_z = set(LOCALS) | {d - parent for d, parent in relays}
    steps_z |= {-d for d in steps_z} | {far_step(ring_z), -far_step(ring_z)}
    friends = [device(dz=d) for d in sorted(steps_z)]
    friends += [device(dy=1), device(dy=-1), device(dy=2), device(dc=1)]
    for j in range(1, reps):
        friends += [device(dr=j), device(dr=j, dc=1)]
    for friend in friends:
        pl.semaphore_signal(barrier, inc=1, device_id=friend, device_id_type=MESH)

    for load in loads[:3]:
        load.wait()
    classes = label_table.shape[0]
    one_hot = (
        lax.broadcasted_iota(jnp.int32, (classes, edge), 0) == class_ids[...]
    ).astype(F32).astype(BF16)
    labels = lax.dot_general(
        one_hot, label_table[...], (((0,), (0,)), ((), ())), preferred_element_type=F32
    )
    inputs = (features[...].astype(F32) + labels).astype(BF16)
    nodes[0] = inputs

    def own_half(whole):
        return jnp.where(core == 0, whole[:, :half_f].astype(F32), whole[:, half_f:].astype(F32)).astype(BF16)

    def gather(layer, whole, work):
        held = chunks[layer]
        top, bottom = slice(0, ROWS_A), slice(ROWS_A, None)
        held[z_slot(0) * RING_Y] = own_half(whole)
        if layer == 0:
            pl.semaphore_wait(barrier, len(friends))

        def at(d, e=0):
            return z_slot(d) * RING_Y + e % RING_Y

        def relay(d, to):
            return send(held.at[at(d)], held.at[at(to)], device(dz=d - to))

        def along_y(d, rows=slice(None)):
            return [
                send(held.at[at(d), rows], held.at[at(d, -dy), rows], device(dy=dy))
                for dy in (2, 1, -1)
            ]

        def spread(d):
            onward = [(to, relay(d, to)) for to, parent in relays if parent == d]
            across = []
            if d == (FAR_FROM if relays else 0):
                across = [
                    send(held.at[at(d)], held.at[at(half_z)], device(dz=far_step(ring_z)))
                ]
            near = [
                (dz, send(held.at[at(d)], held.at[at(d - dz)], device(dz=dz))) for dz in LOCALS
            ]
            side = along_y(d)
            return onward, near, side, across

        last = []

        def corners(d, near, side):
            for dz, copy in near:
                copy.wait_recv()
                last.extend(along_y(d - dz, bottom))
            for copy in side:
                copy.wait_recv()
            for dz in LOCALS:
                last.append(
                    send(
                        held.at[pl.ds(at(d, 1), RING_Y - 1), top],
                        held.at[pl.ds(at(d - dz, 1), RING_Y - 1), top],
                        device(dz=dz),
                    )
                )

        coming, near, side, opposite = spread(0)
        work(0)
        corners(0, near, side)
        work(1)
        pending = []
        while coming:
            d, copy = coming.pop(0)
            copy.wait_recv()
            onward, near, side, across = spread(d)
            coming += onward
            opposite += across
            pending.append((d, near, side))
        for entry in pending[:-2]:
            corners(*entry)
        opposite[0].wait_recv()
        last.extend(along_y(half_z))
        for entry in pending[-2:]:
            corners(*entry)
        for copy in last:
            copy.wait_recv()

    for load in loads[3:]:
        load.wait()
    filled = count[0, 0]
    targets = [(block_row[0, 0, k] - rep + reps) % reps for k in range(slots)]
    per_step = max(slots // 4, 1)
    ones = jnp.ones((per_step * edge, half_f), BF16)
    hidden = []

    def place(step):
        for k in range(step * per_step, (step + 1) * per_step):
            tile = tiles[k]
            for j in range(reps):
                keep = jnp.logical_and(targets[k] == j, k < filled)
                placed[pl.ds(j * edge, edge), pl.ds(k * edge, edge)] = jnp.where(
                    keep, tile, jnp.zeros_like(tile)
                )
        sums = jnp.dot(
            placed[:, pl.ds(step * per_step * edge, per_step * edge)], ones, preferred_element_type=F32
        )
        if step == 0:
            degree[...] = sums
        else:
            degree[...] += sums

    pieces = slots // per_step

    def first_work(at):
        if at == 0:
            hidden.append(send(weights.at[core], weights.at[core], device(dc=1)))
            for piece in range(pieces // 2):
                place(piece)
        if at == 1:
            for piece in range(pieces // 2, pieces):
                place(piece)
            for j in range(1, reps):
                hidden.append(
                    send(degree.at[pl.ds(j * edge, edge)], degree_arrived.at[j - 1], device(dr=j))
                )
            hidden[0].wait_recv()
            own_product[...] = jnp.dot(nodes[0], weights[0, 0], preferred_element_type=F32)

    def second_work(s):
        if s == 1:
            own_product[...] = jnp.dot(nodes[1], weights[1, 0], preferred_element_type=F32)

    def aggregate(layer):
        held = chunks[layer]
        for k in range(slots):
            at = (section[0, 0, k] // RING_Y - z + ring_z + half_z - 1) % ring_z
            e = (section[0, 0, k] % RING_Y - y + RING_Y) % RING_Y
            panels[pl.ds(k * edge, edge), :] = held[at * RING_Y + e]
        copies = []
        for j in [reps // 2] + [j for j in range(1, reps) if j != reps // 2] + [0]:
            total = jnp.dot(
                placed[pl.ds(j * edge, edge), :], panels[...], preferred_element_type=F32
            ).astype(BF16)
            if j == 0:
                arrived[layer, 0, core] = total
            else:
                to_send[layer, j - 1] = total
            if layer == 0:
                if j > 0:
                    source = to_send.at[layer, j - 1]
                    copies.append(send(source, arrived.at[layer, j, core], device(dr=j)))
                else:
                    source = arrived.at[layer, 0, core]
                copies.append(
                    send(source, arrived.at[layer, j, core], device(dr=j, dc=1))
                )
            elif j > 0:
                copies.append(to_second(j))
                copies[-1].start()
        return copies

    def to_second(j, from_core=None):
        from_core = core if from_core is None else from_core
        at = len(started_slots) + 2 * (j - 1)
        return pltpu.make_async_remote_copy(
            src_ref=to_send.at[1, j - 1],
            dst_ref=arrived.at[1, j, from_core],
            send_sem=send_sem.at[at],
            recv_sem=recv_sem.at[at + from_core],
            device_id=(1,) + device(dr=j)[1:],
            device_id_type=MESH,
        )

    def mixture(layer, scale):
        z_sum = own_product[...]
        for c in range(2):
            near = sum(arrived[layer, j, c].astype(F32) for j in range(reps))
            agg = (near * scale).astype(BF16)
            z_sum = z_sum + jnp.dot(
                agg, weights[layer, 1, c * half_f : (c + 1) * half_f, :], preferred_element_type=F32
            )
        return z_sum

    gather(0, inputs, first_work)
    copies = aggregate(0)
    for copy in hidden[1:] + copies:
        copy.wait_recv()
    total_degree = degree[:edge, :]
    for j in range(1, reps):
        total_degree = total_degree + degree_arrived[j - 1]
    degree[:edge, :] = lax.rsqrt(total_degree)
    active = jnp.maximum(mixture(0, degree[:edge, :]), 0.0)
    center = active - jnp.mean(active, axis=-1, keepdims=True)
    spread = jnp.mean(center * center, axis=-1, keepdims=True)
    first = (center * lax.rsqrt(spread + 1e-05) * norm_scale[...]).astype(BF16)
    nodes[1] = first

    gather(1, first, second_work)
    started_slots = list(started)
    copies = aggregate(1)
    last_at = len(started_slots) + 2 * (reps - 1)
    across = pltpu.make_async_remote_copy(
        src_ref=arrived.at[1, 0, 0],
        dst_ref=arrived.at[1, 0, 0],
        send_sem=send_sem.at[last_at],
        recv_sem=recv_sem.at[last_at],
        device_id=(1, row, rep),
        device_id_type=MESH,
    )

    @pl.when(core == 0)
    def _():
        across.start()
        out[0] = nodes[1]
        across.wait_send()

    @pl.when(core == 1)
    def _():
        for j in range(1, reps):
            for c in range(2):
                to_second(j, c).wait_recv()
        across.wait_recv()
        out[0] = mixture(1, degree[:edge, :]).astype(BF16)

    for copy in started_slots + copies:
        copy.wait_send()


def solution(mesh):
    reps = mesh.shape["rep"]
    ring_z = mesh.shape["row"] // RING_Y

    def body(
        features,
        class_ids,
        label_table,
        self_weight,
        neighbor_weight,
        norm_scale,
        tile_values,
        block_row,
        section,
        count,
    ):
        slots, edge = tile_values.shape[2:4]
        width = features.shape[1]
        half = width // 2
        vmem = pl.BlockSpec(memory_space=pltpu.VMEM)
        hbm = pl.BlockSpec(memory_space=pltpu.HBM)
        classes = label_table.shape[0]
        copies = 2 * (3 + 6 * ring_z) + 8 * reps + 16
        return pl.pallas_call(
            functools.partial(kernel, ring_z, reps),
            out_shape=jax.ShapeDtypeStruct((1, edge, width), BF16),
            in_specs=[hbm] * 10,
            out_specs=vmem,
            scratch_shapes=[
                pltpu.VMEM((edge, width), BF16),
                pltpu.VMEM((1, edge), jnp.int32),
                pltpu.VMEM((classes, width), BF16),
                pltpu.VMEM((1, width), F32),
                pltpu.SMEM((1, 1, slots), jnp.int32),
                pltpu.SMEM((1, 1, slots), jnp.int32),
                pltpu.SMEM((1, 1), jnp.int32),
                pltpu.VMEM((slots, edge, edge), BF16),
                pltpu.VMEM((reps * edge, slots * edge), BF16),
                pltpu.VMEM((slots * edge, half), BF16),
                pltpu.VMEM((ring_z * RING_Y, edge, half), BF16),
                pltpu.VMEM((ring_z * RING_Y, edge, half), BF16),
                pltpu.VMEM((2, 2, width, width), BF16),
                pltpu.VMEM((2, edge, width), BF16),
                pltpu.VMEM((edge, width), F32),
                pltpu.VMEM((2, reps - 1, edge, half), BF16),
                pltpu.VMEM((2, reps, 2, edge, half), BF16),
                pltpu.VMEM((reps * edge, half), F32),
                pltpu.VMEM((reps - 1, edge, half), F32),
                pltpu.SemaphoreType.DMA((copies,)),
                pltpu.SemaphoreType.DMA((copies,)),
                pltpu.SemaphoreType.DMA((10,)),
            ],
            compiler_params=pltpu.CompilerParams(
                collective_id=0, has_side_effects=True, vmem_limit_bytes=56442880
            ),
        )(
            features,
            class_ids.reshape(1, edge),
            label_table,
            self_weight,
            neighbor_weight,
            norm_scale.reshape(1, width),
            tile_values,
            block_row,
            section,
            count,
        )

    return jax.shard_map(
        body,
        mesh=mesh,
        in_specs=(
            P(("row", "rep"), None),
            P(("row", "rep")),
            P(),
            P("layer", None, None),
            P("layer", None, None),
            P(),
            P("row", "rep", None, None, None),
            P("row", "rep", None),
            P("row", "rep", None),
            P("row", "rep"),
        ),
        out_specs=P("layer", ("row", "rep"), None),
        check_vma=False,
    )
```

```python
import functools

import jax
import jax.numpy as jnp
from jax import lax
from jax.experimental import pallas as pl
from jax.experimental.pallas import tpu as pltpu
from jax.sharding import PartitionSpec as P

MESH = pl.DeviceIdType.MESH
RING_Y = 4
ROWS_A = 64
RELAYS = [(-3, 0), (3, 0), (-6, -3), (6, 3)]
LOCALS = [1, -1]
FAR_FROM = -6
F32 = jnp.float32
BF16 = jnp.bfloat16


def far_step(ring_z):
    return ring_z // 2 + FAR_FROM if ring_z > 4 else 2


def kernel(
    ring_z,
    reps,
    features_in,
    class_ids_in,
    label_table_in,
    self_weight,
    neighbor_weight,
    norm_scale_in,
    tile_values,
    block_row_in,
    section_in,
    count_in,
    out,
    features,
    class_ids,
    label_table,
    norm_scale,
    block_row,
    section,
    count,
    tiles,
    placed,
    panels,
    first_chunks,
    second_chunks,
    weights,
    nodes,
    own_product,
    to_send,
    arrived,
    degree,
    degree_arrived,
    send_sem,
    recv_sem,
    load_sem,
):
    slots = tiles.shape[0]
    edge = tiles.shape[1]
    chunks = (first_chunks, second_chunks)
    half_f = first_chunks.shape[-1]
    half_z = ring_z // 2
    core = lax.axis_index("layer")
    row = lax.axis_index("row")
    rep = lax.axis_index("rep")
    z, y = row // RING_Y, row % RING_Y

    def device(dz=0, dy=0, dr=0, dc=0):
        to_row = ((z + dz + ring_z) % ring_z) * RING_Y + (y + dy + RING_Y) % RING_Y
        return ((core + dc) % 2, to_row, (rep + dr) % reps)

    def z_slot(d):
        return (d + half_z - 1) % ring_z

    started = []

    def send(src, dst, device_id):
        at = len(started)
        copy = pltpu.make_async_remote_copy(
            src_ref=src,
            dst_ref=dst,
            send_sem=send_sem.at[at],
            recv_sem=recv_sem.at[at],
            device_id=device_id,
            device_id_type=MESH,
        )
        copy.start()
        started.append(copy)
        return copy

    loads = [
        pltpu.make_async_copy(src, dst, load_sem.at[i])
        for i, (src, dst) in enumerate(
            [
                (class_ids_in, class_ids),
                (label_table_in, label_table),
                (features_in, features),
                (block_row_in, block_row),
                (section_in, section),
                (count_in, count),
                (norm_scale_in, norm_scale),
                (tile_values.at[0, 0], tiles),
                (self_weight.at[0], weights.at[core, 0]),
                (neighbor_weight.at[0], weights.at[core, 1]),
            ]
        )
    ]
    for load in loads:
        load.start()

    barrier = pltpu.get_barrier_semaphore()
    relays = RELAYS if ring_z > 4 else []
    steps_z = set(LOCALS) | {d - parent for d, parent in relays}
    steps_z |= {-d for d in steps_z} | {far_step(ring_z), -far_step(ring_z)}
    friends = [device(dz=d) for d in sorted(steps_z)]
    friends += [device(dy=1), device(dy=-1), device(dy=2), device(dc=1)]
    for j in range(1, reps):
        friends += [device(dr=j), device(dr=j, dc=1)]
    for friend in friends:
        pl.semaphore_signal(barrier, inc=1, device_id=friend, device_id_type=MESH)

    for load in loads[:3]:
        load.wait()
    classes = label_table.shape[0]
    one_hot = (
        lax.broadcasted_iota(jnp.int32, (classes, edge), 0) == class_ids[...]
    ).astype(F32).astype(BF16)
    labels = lax.dot_general(
        one_hot, label_table[...], (((0,), (0,)), ((), ())), preferred_element_type=F32
    )
    inputs = (features[...].astype(F32) + labels).astype(BF16)
    nodes[0] = inputs

    def own_half(whole):
        return jnp.where(core == 0, whole[:, :half_f].astype(F32), whole[:, half_f:].astype(F32)).astype(BF16)

    def gather(layer, whole, work):
        held = chunks[layer]
        top, bottom = slice(0, ROWS_A), slice(ROWS_A, None)
        held[z_slot(0) * RING_Y] = own_half(whole)
        if layer == 0:
            pl.semaphore_wait(barrier, len(friends))

        def at(d, e=0):
            return z_slot(d) * RING_Y + e % RING_Y

        def relay(d, to):
            return send(held.at[at(d)], held.at[at(to)], device(dz=d - to))

        def along_y(d, rows=slice(None)):
            return [
                send(held.at[at(d), rows], held.at[at(d, -dy), rows], device(dy=dy))
                for dy in (2, 1, -1)
            ]

        def spread(d):
            onward = [(to, relay(d, to)) for to, parent in relays if parent == d]
            across = []
            if d == (FAR_FROM if relays else 0):
                across = [
                    send(held.at[at(d)], held.at[at(half_z)], device(dz=far_step(ring_z)))
                ]
            near = [
                (dz, send(held.at[at(d)], held.at[at(d - dz)], device(dz=dz))) for dz in LOCALS
            ]
            side = along_y(d)
            return onward, near, side, across

        last = []

        def corners(d, near, side):
            for dz, copy in near:
                copy.wait_recv()
                last.extend(along_y(d - dz, bottom))
            for copy in side:
                copy.wait_recv()
            for dz in LOCALS:
                last.append(
                    send(
                        held.at[pl.ds(at(d, 1), RING_Y - 1), top],
                        held.at[pl.ds(at(d - dz, 1), RING_Y - 1), top],
                        device(dz=dz),
                    )
                )

        coming, near, side, opposite = spread(0)
        work(0)
        corners(0, near, side)
        work(1)
        pending = []
        while coming:
            d, copy = coming.pop(0)
            copy.wait_recv()
            onward, near, side, across = spread(d)
            coming += onward
            opposite += across
            pending.append((d, near, side))
        for entry in pending[:-2]:
            corners(*entry)
        opposite[0].wait_recv()
        last.extend(along_y(half_z))
        for entry in pending[-2:]:
            corners(*entry)
        for copy in last:
            copy.wait_recv()

    filled, targets = [], []
    per_step = max(slots // 4, 1)
    ones = jnp.ones((per_step * edge, half_f), BF16)
    hidden = []

    def place(step):
        for k in range(step * per_step, (step + 1) * per_step):
            tile = tiles[k]
            for j in range(reps):
                keep = jnp.logical_and(targets[k] == j, k < filled[0])
                placed[pl.ds(j * edge, edge), pl.ds(k * edge, edge)] = jnp.where(
                    keep, tile, jnp.zeros_like(tile)
                )
        sums = jnp.dot(
            placed[:, pl.ds(step * per_step * edge, per_step * edge)], ones, preferred_element_type=F32
        )
        if step == 0:
            degree[...] = sums
        else:
            degree[...] += sums

    pieces = slots // per_step

    def first_work(at):
        if at == 0:
            for load in loads[3:]:
                load.wait()
            filled.append(count[0, 0])
            targets.extend((block_row[0, 0, k] - rep + reps) % reps for k in range(slots))
            hidden.append(send(weights.at[core], weights.at[core], device(dc=1)))
            for piece in range(pieces // 2):
                place(piece)
        if at == 1:
            for piece in range(pieces // 2, pieces):
                place(piece)
            for j in range(1, reps):
                hidden.append(
                    send(degree.at[pl.ds(j * edge, edge)], degree_arrived.at[j - 1], device(dr=j))
                )
            hidden[0].wait_recv()
            own_product[...] = jnp.dot(nodes[0], weights[0, 0], preferred_element_type=F32)

    def second_work(s):
        if s == 1:
            own_product[...] = jnp.dot(nodes[1], weights[1, 0], preferred_element_type=F32)

    def aggregate(layer):
        held = chunks[layer]
        for k in range(slots):
            at = (section[0, 0, k] // RING_Y - z + ring_z + half_z - 1) % ring_z
            e = (section[0, 0, k] % RING_Y - y + RING_Y) % RING_Y
            panels[pl.ds(k * edge, edge), :] = held[at * RING_Y + e]
        copies = []
        for j in [reps // 2] + [j for j in range(1, reps) if j != reps // 2] + [0]:
            total = jnp.dot(
                placed[pl.ds(j * edge, edge), :], panels[...], preferred_element_type=F32
            ).astype(BF16)
            if j == 0:
                arrived[layer, 0, core] = total
            else:
                to_send[layer, j - 1] = total
            if layer == 0:
                if j > 0:
                    source = to_send.at[layer, j - 1]
                    copies.append(send(source, arrived.at[layer, j, core], device(dr=j)))
                else:
                    source = arrived.at[layer, 0, core]
                copies.append(
                    send(source, arrived.at[layer, j, core], device(dr=j, dc=1))
                )
            elif j > 0:
                copies.append(to_second(j))
                copies[-1].start()
        return copies

    def to_second(j, from_core=None):
        from_core = core if from_core is None else from_core
        at = len(started_slots) + 2 * (j - 1)
        return pltpu.make_async_remote_copy(
            src_ref=to_send.at[1, j - 1],
            dst_ref=arrived.at[1, j, from_core],
            send_sem=send_sem.at[at],
            recv_sem=recv_sem.at[at + from_core],
            device_id=(1,) + device(dr=j)[1:],
            device_id_type=MESH,
        )

    def mixture(layer, scale):
        z_sum = own_product[...]
        for c in range(2):
            near = sum(arrived[layer, j, c].astype(F32) for j in range(reps))
            agg = (near * scale).astype(BF16)
            z_sum = z_sum + jnp.dot(
                agg, weights[layer, 1, c * half_f : (c + 1) * half_f, :], preferred_element_type=F32
            )
        return z_sum

    gather(0, inputs, first_work)
    copies = aggregate(0)
    for copy in hidden[1:] + copies:
        copy.wait_recv()
    total_degree = degree[:edge, :]
    for j in range(1, reps):
        total_degree = total_degree + degree_arrived[j - 1]
    degree[:edge, :] = lax.rsqrt(total_degree)
    active = jnp.maximum(mixture(0, degree[:edge, :]), 0.0)
    center = active - jnp.mean(active, axis=-1, keepdims=True)
    spread = jnp.mean(center * center, axis=-1, keepdims=True)
    first = (center * lax.rsqrt(spread + 1e-05) * norm_scale[...]).astype(BF16)
    nodes[1] = first

    gather(1, first, second_work)
    started_slots = list(started)
    copies = aggregate(1)
    last_at = len(started_slots) + 2 * (reps - 1)
    across = pltpu.make_async_remote_copy(
        src_ref=arrived.at[1, 0, 0],
        dst_ref=arrived.at[1, 0, 0],
        send_sem=send_sem.at[last_at],
        recv_sem=recv_sem.at[last_at],
        device_id=(1, row, rep),
        device_id_type=MESH,
    )

    @pl.when(core == 0)
    def _():
        across.start()
        out[0] = nodes[1]
        across.wait_send()

    @pl.when(core == 1)
    def _():
        for j in range(1, reps):
            for c in range(2):
                to_second(j, c).wait_recv()
        across.wait_recv()
        out[0] = mixture(1, degree[:edge, :]).astype(BF16)

    for copy in started_slots + copies:
        copy.wait_send()


def solution(mesh):
    reps = mesh.shape["rep"]
    ring_z = mesh.shape["row"] // RING_Y

    def body(
        features,
        class_ids,
        label_table,
        self_weight,
        neighbor_weight,
        norm_scale,
        tile_values,
        block_row,
        section,
        count,
    ):
        slots, edge = tile_values.shape[2:4]
        width = features.shape[1]
        half = width // 2
        vmem = pl.BlockSpec(memory_space=pltpu.VMEM)
        hbm = pl.BlockSpec(memory_space=pltpu.HBM)
        classes = label_table.shape[0]
        copies = 2 * (3 + 6 * ring_z) + 8 * reps + 16
        return pl.pallas_call(
            functools.partial(kernel, ring_z, reps),
            out_shape=jax.ShapeDtypeStruct((1, edge, width), BF16),
            in_specs=[hbm] * 10,
            out_specs=vmem,
            scratch_shapes=[
                pltpu.VMEM((edge, width), BF16),
                pltpu.VMEM((1, edge), jnp.int32),
                pltpu.VMEM((classes, width), BF16),
                pltpu.VMEM((1, width), F32),
                pltpu.SMEM((1, 1, slots), jnp.int32),
                pltpu.SMEM((1, 1, slots), jnp.int32),
                pltpu.SMEM((1, 1), jnp.int32),
                pltpu.VMEM((slots, edge, edge), BF16),
                pltpu.VMEM((reps * edge, slots * edge), BF16),
                pltpu.VMEM((slots * edge, half), BF16),
                pltpu.VMEM((ring_z * RING_Y, edge, half), BF16),
                pltpu.VMEM((ring_z * RING_Y, edge, half), BF16),
                pltpu.VMEM((2, 2, width, width), BF16),
                pltpu.VMEM((2, edge, width), BF16),
                pltpu.VMEM((edge, width), F32),
                pltpu.VMEM((2, reps - 1, edge, half), BF16),
                pltpu.VMEM((2, reps, 2, edge, half), BF16),
                pltpu.VMEM((reps * edge, half), F32),
                pltpu.VMEM((reps - 1, edge, half), F32),
                pltpu.SemaphoreType.DMA((copies,)),
                pltpu.SemaphoreType.DMA((copies,)),
                pltpu.SemaphoreType.DMA((10,)),
            ],
            compiler_params=pltpu.CompilerParams(
                collective_id=0, has_side_effects=True, vmem_limit_bytes=56442880
            ),
        )(
            features,
            class_ids.reshape(1, edge),
            label_table,
            self_weight,
            neighbor_weight,
            norm_scale.reshape(1, width),
            tile_values,
            block_row,
            section,
            count,
        )

    return jax.shard_map(
        body,
        mesh=mesh,
        in_specs=(
            P(("row", "rep"), None),
            P(("row", "rep")),
            P(),
            P("layer", None, None),
            P("layer", None, None),
            P(),
            P("row", "rep", None, None, None),
            P("row", "rep", None),
            P("row", "rep", None),
            P("row", "rep"),
        ),
        out_specs=P("layer", ("row", "rep"), None),
        check_vma=False,
    )
```

```python
import functools

import jax
import jax.numpy as jnp
from jax import lax
from jax.experimental import pallas as pl
from jax.experimental.pallas import tpu as pltpu
from jax.sharding import PartitionSpec as P

MESH = pl.DeviceIdType.MESH
RING_Y = 4
ROWS_A = 80
RELAYS = [(-3, 0), (3, 0), (-6, -3), (6, 3)]
LOCALS = [1, -1]
FAR_FROM = -6
F32 = jnp.float32
BF16 = jnp.bfloat16


def far_step(ring_z):
    return ring_z // 2 + FAR_FROM if ring_z > 4 else 2


def kernel(
    ring_z,
    reps,
    features_in,
    class_ids_in,
    label_table_in,
    self_weight,
    neighbor_weight,
    norm_scale_in,
    tile_values,
    block_row_in,
    section_in,
    count_in,
    out,
    features,
    class_ids,
    label_table,
    norm_scale,
    block_row,
    section,
    count,
    tiles,
    placed,
    panels,
    first_chunks,
    second_chunks,
    weights,
    nodes,
    own_product,
    to_send,
    arrived,
    degree,
    degree_arrived,
    send_sem,
    recv_sem,
    load_sem,
):
    slots = tiles.shape[0]
    edge = tiles.shape[1]
    chunks = (first_chunks, second_chunks)
    half_f = first_chunks.shape[-1]
    half_z = ring_z // 2
    core = lax.axis_index("layer")
    row = lax.axis_index("row")
    rep = lax.axis_index("rep")
    z, y = row // RING_Y, row % RING_Y

    def device(dz=0, dy=0, dr=0, dc=0):
        to_row = ((z + dz + ring_z) % ring_z) * RING_Y + (y + dy + RING_Y) % RING_Y
        return ((core + dc) % 2, to_row, (rep + dr) % reps)

    def z_slot(d):
        return (d + half_z - 1) % ring_z

    started = []

    def send(src, dst, device_id):
        at = len(started)
        copy = pltpu.make_async_remote_copy(
            src_ref=src,
            dst_ref=dst,
            send_sem=send_sem.at[at],
            recv_sem=recv_sem.at[at],
            device_id=device_id,
            device_id_type=MESH,
        )
        copy.start()
        started.append(copy)
        return copy

    loads = [
        pltpu.make_async_copy(src, dst, load_sem.at[i])
        for i, (src, dst) in enumerate(
            [
                (class_ids_in, class_ids),
                (label_table_in, label_table),
                (features_in, features),
                (block_row_in, block_row),
                (section_in, section),
                (count_in, count),
                (norm_scale_in, norm_scale),
                (tile_values.at[0, 0], tiles),
                (self_weight.at[0], weights.at[core, 0]),
                (neighbor_weight.at[0], weights.at[core, 1]),
            ]
        )
    ]
    for load in loads:
        load.start()

    barrier = pltpu.get_barrier_semaphore()
    relays = RELAYS if ring_z > 4 else []
    steps_z = set(LOCALS) | {d - parent for d, parent in relays}
    steps_z |= {-d for d in steps_z} | {far_step(ring_z), -far_step(ring_z)}
    friends = [device(dz=d) for d in sorted(steps_z)]
    friends += [device(dy=1), device(dy=-1), device(dy=2), device(dc=1)]
    for j in range(1, reps):
        friends += [device(dr=j), device(dr=j, dc=1)]
    for friend in friends:
        pl.semaphore_signal(barrier, inc=1, device_id=friend, device_id_type=MESH)

    for load in loads[:3]:
        load.wait()
    classes = label_table.shape[0]
    one_hot = (
        lax.broadcasted_iota(jnp.int32, (classes, edge), 0) == class_ids[...]
    ).astype(F32).astype(BF16)
    labels = lax.dot_general(
        one_hot, label_table[...], (((0,), (0,)), ((), ())), preferred_element_type=F32
    )
    inputs = (features[...].astype(F32) + labels).astype(BF16)
    nodes[0] = inputs

    def own_half(whole):
        return jnp.where(core == 0, whole[:, :half_f].astype(F32), whole[:, half_f:].astype(F32)).astype(BF16)

    def gather(layer, whole, work):
        held = chunks[layer]
        top, bottom = slice(0, ROWS_A), slice(ROWS_A, None)
        held[z_slot(0) * RING_Y] = own_half(whole)
        if layer == 0:
            pl.semaphore_wait(barrier, len(friends))

        def at(d, e=0):
            return z_slot(d) * RING_Y + e % RING_Y

        def relay(d, to):
            return send(held.at[at(d)], held.at[at(to)], device(dz=d - to))

        def along_y(d, rows=slice(None)):
            return [
                send(held.at[at(d), rows], held.at[at(d, -dy), rows], device(dy=dy))
                for dy in (2, 1, -1)
            ]

        def spread(d):
            onward = [(to, relay(d, to)) for to, parent in relays if parent == d]
            across = []
            if d == (FAR_FROM if relays else 0):
                across = [
                    send(held.at[at(d)], held.at[at(half_z)], device(dz=far_step(ring_z)))
                ]
            near = [
                (dz, send(held.at[at(d)], held.at[at(d - dz)], device(dz=dz))) for dz in LOCALS
            ]
            side = along_y(d)
            return onward, near, side, across

        last = []

        def corners(d, near, side):
            for dz, copy in near:
                copy.wait_recv()
                last.extend(along_y(d - dz, bottom))
            for copy in side:
                copy.wait_recv()
            for dz in LOCALS:
                last.append(
                    send(
                        held.at[pl.ds(at(d, 1), RING_Y - 1), top],
                        held.at[pl.ds(at(d - dz, 1), RING_Y - 1), top],
                        device(dz=dz),
                    )
                )

        coming, near, side, opposite = spread(0)
        work(0)
        corners(0, near, side)
        work(1)
        pending = []
        while coming:
            d, copy = coming.pop(0)
            copy.wait_recv()
            onward, near, side, across = spread(d)
            coming += onward
            opposite += across
            pending.append((d, near, side))
        for entry in pending[:-2]:
            corners(*entry)
        opposite[0].wait_recv()
        last.extend(along_y(half_z))
        for entry in pending[-2:]:
            corners(*entry)
        for copy in last:
            copy.wait_recv()

    filled, targets = [], []
    per_step = max(slots // 4, 1)
    ones = jnp.ones((per_step * edge, half_f), BF16)
    hidden = []

    def place(step):
        for k in range(step * per_step, (step + 1) * per_step):
            tile = tiles[k]
            for j in range(reps):
                keep = jnp.logical_and(targets[k] == j, k < filled[0])
                placed[pl.ds(j * edge, edge), pl.ds(k * edge, edge)] = jnp.where(
                    keep, tile, jnp.zeros_like(tile)
                )
        sums = jnp.dot(
            placed[:, pl.ds(step * per_step * edge, per_step * edge)], ones, preferred_element_type=F32
        )
        if step == 0:
            degree[...] = sums
        else:
            degree[...] += sums

    pieces = slots // per_step

    def first_work(at):
        if at == 0:
            for load in loads[3:]:
                load.wait()
            filled.append(count[0, 0])
            targets.extend((block_row[0, 0, k] - rep + reps) % reps for k in range(slots))
            hidden.append(send(weights.at[core], weights.at[core], device(dc=1)))
            for piece in range(pieces // 2):
                place(piece)
        if at == 1:
            for piece in range(pieces // 2, pieces):
                place(piece)
            for j in range(1, reps):
                hidden.append(
                    send(degree.at[pl.ds(j * edge, edge)], degree_arrived.at[j - 1], device(dr=j))
                )
            hidden[0].wait_recv()
            own_product[...] = jnp.dot(nodes[0], weights[0, 0], preferred_element_type=F32)

    def second_work(s):
        if s == 1:
            own_product[...] = jnp.dot(nodes[1], weights[1, 0], preferred_element_type=F32)

    def aggregate(layer):
        held = chunks[layer]
        for k in range(slots):
            at = (section[0, 0, k] // RING_Y - z + ring_z + half_z - 1) % ring_z
            e = (section[0, 0, k] % RING_Y - y + RING_Y) % RING_Y
            panels[pl.ds(k * edge, edge), :] = held[at * RING_Y + e]
        copies = []
        for j in [reps // 2] + [j for j in range(1, reps) if j != reps // 2] + [0]:
            total = jnp.dot(
                placed[pl.ds(j * edge, edge), :], panels[...], preferred_element_type=F32
            ).astype(BF16)
            if j == 0:
                arrived[layer, 0, core] = total
            else:
                to_send[layer, j - 1] = total
            if layer == 0:
                if j > 0:
                    source = to_send.at[layer, j - 1]
                    copies.append(send(source, arrived.at[layer, j, core], device(dr=j)))
                else:
                    source = arrived.at[layer, 0, core]
                copies.append(
                    send(source, arrived.at[layer, j, core], device(dr=j, dc=1))
                )
            elif j > 0:
                copies.append(to_second(j))
                copies[-1].start()
        return copies

    def to_second(j, from_core=None):
        from_core = core if from_core is None else from_core
        at = len(started_slots) + 2 * (j - 1)
        return pltpu.make_async_remote_copy(
            src_ref=to_send.at[1, j - 1],
            dst_ref=arrived.at[1, j, from_core],
            send_sem=send_sem.at[at],
            recv_sem=recv_sem.at[at + from_core],
            device_id=(1,) + device(dr=j)[1:],
            device_id_type=MESH,
        )

    def mixture(layer, scale):
        z_sum = own_product[...]
        for c in range(2):
            near = sum(arrived[layer, j, c].astype(F32) for j in range(reps))
            agg = (near * scale).astype(BF16)
            z_sum = z_sum + jnp.dot(
                agg, weights[layer, 1, c * half_f : (c + 1) * half_f, :], preferred_element_type=F32
            )
        return z_sum

    gather(0, inputs, first_work)
    copies = aggregate(0)
    for copy in hidden[1:] + copies:
        copy.wait_recv()
    total_degree = degree[:edge, :]
    for j in range(1, reps):
        total_degree = total_degree + degree_arrived[j - 1]
    degree[:edge, :] = lax.rsqrt(total_degree)
    active = jnp.maximum(mixture(0, degree[:edge, :]), 0.0)
    center = active - jnp.mean(active, axis=-1, keepdims=True)
    spread = jnp.mean(center * center, axis=-1, keepdims=True)
    first = (center * lax.rsqrt(spread + 1e-05) * norm_scale[...]).astype(BF16)
    nodes[1] = first

    gather(1, first, second_work)
    started_slots = list(started)
    copies = aggregate(1)
    last_at = len(started_slots) + 2 * (reps - 1)
    across = pltpu.make_async_remote_copy(
        src_ref=arrived.at[1, 0, 0],
        dst_ref=arrived.at[1, 0, 0],
        send_sem=send_sem.at[last_at],
        recv_sem=recv_sem.at[last_at],
        device_id=(1, row, rep),
        device_id_type=MESH,
    )

    @pl.when(core == 0)
    def _():
        across.start()
        out[0] = nodes[1]
        across.wait_send()

    @pl.when(core == 1)
    def _():
        for j in range(1, reps):
            for c in range(2):
                to_second(j, c).wait_recv()
        across.wait_recv()
        out[0] = mixture(1, degree[:edge, :]).astype(BF16)

    for copy in started_slots + copies:
        copy.wait_send()


def solution(mesh):
    reps = mesh.shape["rep"]
    ring_z = mesh.shape["row"] // RING_Y

    def body(
        features,
        class_ids,
        label_table,
        self_weight,
        neighbor_weight,
        norm_scale,
        tile_values,
        block_row,
        section,
        count,
    ):
        slots, edge = tile_values.shape[2:4]
        width = features.shape[1]
        half = width // 2
        vmem = pl.BlockSpec(memory_space=pltpu.VMEM)
        hbm = pl.BlockSpec(memory_space=pltpu.HBM)
        classes = label_table.shape[0]
        copies = 2 * (3 + 6 * ring_z) + 8 * reps + 16
        return pl.pallas_call(
            functools.partial(kernel, ring_z, reps),
            out_shape=jax.ShapeDtypeStruct((1, edge, width), BF16),
            in_specs=[hbm] * 10,
            out_specs=vmem,
            scratch_shapes=[
                pltpu.VMEM((edge, width), BF16),
                pltpu.VMEM((1, edge), jnp.int32),
                pltpu.VMEM((classes, width), BF16),
                pltpu.VMEM((1, width), F32),
                pltpu.SMEM((1, 1, slots), jnp.int32),
                pltpu.SMEM((1, 1, slots), jnp.int32),
                pltpu.SMEM((1, 1), jnp.int32),
                pltpu.VMEM((slots, edge, edge), BF16),
                pltpu.VMEM((reps * edge, slots * edge), BF16),
                pltpu.VMEM((slots * edge, half), BF16),
                pltpu.VMEM((ring_z * RING_Y, edge, half), BF16),
                pltpu.VMEM((ring_z * RING_Y, edge, half), BF16),
                pltpu.VMEM((2, 2, width, width), BF16),
                pltpu.VMEM((2, edge, width), BF16),
                pltpu.VMEM((edge, width), F32),
                pltpu.VMEM((2, reps - 1, edge, half), BF16),
                pltpu.VMEM((2, reps, 2, edge, half), BF16),
                pltpu.VMEM((reps * edge, half), F32),
                pltpu.VMEM((reps - 1, edge, half), F32),
                pltpu.SemaphoreType.DMA((copies,)),
                pltpu.SemaphoreType.DMA((copies,)),
                pltpu.SemaphoreType.DMA((10,)),
            ],
            compiler_params=pltpu.CompilerParams(
                collective_id=0, has_side_effects=True, vmem_limit_bytes=56442880
            ),
        )(
            features,
            class_ids.reshape(1, edge),
            label_table,
            self_weight,
            neighbor_weight,
            norm_scale.reshape(1, width),
            tile_values,
            block_row,
            section,
            count,
        )

    return jax.shard_map(
        body,
        mesh=mesh,
        in_specs=(
            P(("row", "rep"), None),
            P(("row", "rep")),
            P(),
            P("layer", None, None),
            P("layer", None, None),
            P(),
            P("row", "rep", None, None, None),
            P("row", "rep", None),
            P("row", "rep", None),
            P("row", "rep"),
        ),
        out_specs=P("layer", ("row", "rep"), None),
        check_vma=False,
    )
```
